512 devices in a mesh: seq: 64 (over y, z), mp: 8 (over x, core).
Axes of the slice: x: 4, y: 8, z: 8, core: 2. Of those that a mesh axis runs over, the one named last changes fastest.
Arguments:
- inputs: bfloat16 [40960, 6144], P('seq', 'mp'), may hold values from -6 to 6
- queries: bfloat16 [40960, 4096], P('seq', 'mp'), may hold values from -12 to 12
- key_rows: bfloat16 [40960, 4096], P('seq', 'mp'), may hold values from -12 to 12
- values: bfloat16 [40960, 4096], P('seq', 'mp'), may hold values from -6 to 6
- norm_gain: float32 [4096], P('mp'), may hold values from 0.1 to 1.9
- cotangent: bfloat16 [40960, 4096], P('seq', 'mp'), may hold values from -6 to 6
- adapter_down: float32 [32, 6144], P(None, 'mp'), may hold values from -6 to 6
- adapter_up: float32 [32, 4096], P(None, 'mp'), may hold values from -6 to 6
- moment_down: float32 [32, 6144], P(None, 'mp'), may hold values from -6 to 6
- moment_up: float32 [32, 4096], P(None, 'mp'), may hold values from -6 to 6
- noise_down: float32 [32, 6144], P(None, 'mp'), may hold values from -6 to 6
- noise_up: float32 [32, 4096], P(None, 'mp'), may hold values from -6 to 6
Outputs:
- normed: bfloat16 [40960, 4096], P('seq', 'mp')
- new_down: float32 [32, 6144], P(None, 'mp')
- new_moment_down: float32 [32, 6144], P(None, 'mp')
- new_up: float32 [32, 4096], P(None, 'mp')
- new_moment_up: float32 [32, 4096], P(None, 'mp')
The draws below stay inside these ranges and needn't reach their ends.
All inputs are finite; a program needn't handle non-finite values.
Results may differ from the reference program's by a relative error of at most 0.007.
Values sent between devices are 32-bit elements; how exact they have to be, the bound alone decides.
A program may use at most 128 MiB of HBM per device.

```python
import math
import jax
import jax.numpy as jnp
from jax import lax

D = 6144
HEADS = 32
HEAD = 128
RANK = 32
TOK = 640
STEP = 250
CYCLE = 1000
SEQ = 40960
HC = 4096
N_SEQ = 64


def block_scale(key, extent, cuts, least, top_value):
    def one(axis_at, shards_of):
        heights = jax.random.uniform(jax.random.fold_in(jax.random.fold_in(key, 6), axis_at), (shards_of,), jnp.float32, least / len(cuts), top_value / len(cuts))
        return jnp.repeat(jnp.exp(heights), extent[axis_at] // shards_of).reshape((-1,) + (1,) * (len(extent) - axis_at - 1))

    level = one(*cuts[0])
    for cut in cuts[1:]:
        level = level * one(*cut)
    return level


def centred(own_key, dims, scale, limit, cuts=(), held_as=jnp.bfloat16):
    result = jax.random.normal(own_key, dims, jnp.float32) * scale
    if len(cuts) > 0:
        result = block_scale(own_key, dims, cuts, -0.22, 0.18) * result
    return jnp.clip(result, min=-limit, max=limit).astype(held_as)


def setup_inputs(seed: int = 0) -> dict:
    keys = jax.random.split(jax.random.key(seed), 13)
    return {
        "inputs": centred(keys[0], (SEQ, D), 1.0, 6.0, ((0, 64), (1, 8))),
        "queries": centred(keys[1], (SEQ, HC), 2.0, 12.0, ((0, 64), (1, 8))),
        "key_rows": centred(keys[2], (SEQ, HC), 2.0, 12.0, ((0, 64), (1, 8))),
        "values": centred(keys[3], (SEQ, HC), 1.0, 6.0, ((0, 64), (1, 8))),
        "norm_gain": jnp.clip(1.0 + 0.18 * jax.random.normal(keys[4], (HC,), jnp.float32), 0.1, 1.9),
        "cotangent": centred(keys[5], (SEQ, HC), 1.0, 6.0, ((0, 64), (1, 8))),
        "adapter_down": centred(keys[6], (RANK, D), 1.0, 6.0, ((1, 8),), jnp.float32),
        "adapter_up": centred(keys[7], (RANK, HC), 1.0, 6.0, ((1, 8),), jnp.float32),
        "moment_down": centred(keys[8], (RANK, D), 1.0, 6.0, ((1, 8),), jnp.float32),
        "moment_up": centred(keys[9], (RANK, HC), 1.0, 6.0, ((1, 8),), jnp.float32),
        "noise_down": centred(keys[10], (RANK, D), 1.0, 6.0, ((1, 8),), jnp.float32),
        "noise_up": centred(keys[11], (RANK, HC), 1.0, 6.0, ((1, 8),), jnp.float32),
    }


friction = 0.2
peak_rate = 0.03
epsilon = 1e-06

def round_half(array):
    return lax.optimization_barrier(array.astype(jnp.bfloat16)).astype(jnp.float32)

def feature_map(array):
    return (jax.nn.elu(array.astype(jnp.float32)) + 1.0).astype(jnp.bfloat16)

def sghmc_step(parameter, moment, gradient, noise_term):
    step_rate = peak_rate * (math.cos(math.pi * ((STEP - 1) % CYCLE) / CYCLE) + 1.0)
    spread = math.sqrt(2.0 * friction * step_rate)
    moment_new = (1.0 - friction) * moment - step_rate * gradient + spread * noise_term
    return (parameter + moment_new, moment_new)

def reference(inputs, queries, key_rows, values, norm_gain, cotangent, adapter_down, adapter_up, moment_down, moment_up, noise_down, noise_up):
    down_half = adapter_down.astype(jnp.bfloat16)
    up_half = adapter_up.astype(jnp.bfloat16)
    inner_sum = jnp.dot(inputs, down_half.T, preferred_element_type=jnp.float32) / math.sqrt(D)
    inner_half = inner_sum.astype(jnp.bfloat16)
    lifted = jnp.dot(inner_half, up_half, preferred_element_type=jnp.float32) / math.sqrt(RANK)
    value_mix = (values.astype(jnp.float32) + lifted).astype(jnp.bfloat16)
    query_feat = feature_map(queries)
    key_feat = feature_map(key_rows)
    blocked = (N_SEQ, TOK, HEADS, HEAD)
    query_blocks = query_feat.reshape(blocked).astype(jnp.float32)
    key_blocks = key_feat.reshape(blocked).astype(jnp.float32)
    value_blocks = value_mix.reshape(blocked).astype(jnp.float32)
    cot_blocks = cotangent.reshape(blocked).astype(jnp.float32)
    gain_rows = norm_gain.reshape(HEADS, HEAD)
    states = jnp.einsum('cthd,cthe->chde', key_blocks, value_blocks)
    running = jnp.cumsum(states, axis=0)
    prefix = jnp.concatenate([jnp.zeros_like(states[:1]), running[:-1]], axis=0)
    positions = jnp.arange(TOK, dtype=jnp.int32)
    causal = positions[:, None] >= positions[None, :]

    def one_block(pieces):
        query_rows, key_block, value_rows, prefix_rows, cot_rows = pieces
        scores = jnp.einsum('thd,shd->hts', query_rows, key_block)
        weights = round_half(jnp.where(causal[None], scores, 0.0))
        nearby = jnp.einsum('hts,she->the', weights, value_rows)
        carried = jnp.einsum('thd,hde->the', query_rows, round_half(prefix_rows))
        summed = nearby + carried
        inverse_norm = lax.rsqrt(lax.optimization_barrier(jnp.mean(summed * summed, axis=-1, keepdims=True)) + epsilon)
        unit_rows = summed * inverse_norm
        normed = (gain_rows * unit_rows).astype(jnp.bfloat16)
        gain_grad = gain_rows * cot_rows
        projected = lax.optimization_barrier(jnp.mean(gain_grad * unit_rows, axis=-1, keepdims=True))
        out_grad = round_half(inverse_norm * (gain_grad - unit_rows * projected))
        back_states = jnp.einsum('thd,the->hde', query_rows, out_grad)
        grad_near = jnp.einsum('hts,the->she', weights, out_grad)
        return (normed, back_states, grad_near)
    normed, back_states, grad_near = lax.map(one_block, (query_blocks, key_blocks, value_blocks, prefix, cot_blocks))
    tail_sums = jnp.cumsum(back_states[::-1], axis=0)[::-1]
    suffix = jnp.concatenate([tail_sums[1:], jnp.zeros_like(back_states[:1])], axis=0)
    grad_values = grad_near + jnp.einsum('cshd,chde->cshe', key_blocks, round_half(suffix))
    grad_half = grad_values.astype(jnp.bfloat16).reshape(SEQ, HC)
    inner_grad = jnp.dot(grad_half, up_half.T, preferred_element_type=jnp.float32) / math.sqrt(RANK)
    inner_grad_half = inner_grad.astype(jnp.bfloat16)
    grad_down = jnp.dot(inner_grad_half.T, inputs, preferred_element_type=jnp.float32) / math.sqrt(D)
    grad_up = jnp.dot(inner_half.T, grad_half, preferred_element_type=jnp.float32) / math.sqrt(RANK)
    new_down, new_moment_down = sghmc_step(adapter_down, moment_down, grad_down, noise_down)
    new_up, new_moment_up = sghmc_step(adapter_up, moment_up, grad_up, noise_up)
    return (normed.reshape(SEQ, HC), new_down, new_moment_down, new_up, new_moment_up)
```

```python
import functools
import math

import jax
import jax.numpy as jnp
from jax import lax
from jax.experimental import pallas as pl
from jax.experimental.pallas import tpu as pltpu
from jax.sharding import PartitionSpec as P

D = 6144
HEAD = 128
RANK = 32
STEP = 250
CYCLE = 1000
TOK = 640
HEADS = 4
COLS = HEADS * HEAD
FEATS = 768
CHUNK = 128
CHUNKS = TOK // CHUNK
SIDE = 8
MESH = pl.DeviceIdType.MESH

friction = 0.2
peak_rate = 0.03
epsilon = 1e-06
step_rate = peak_rate * (math.cos(math.pi * ((STEP - 1) % CYCLE) / CYCLE) + 1.0)
spread = math.sqrt(2.0 * friction * step_rate)

F32 = jnp.float32
BF16 = jnp.bfloat16


def dot(a, b, ca, cb):
    return lax.dot_general(a, b, (((ca,), (cb,)), ((), ())), preferred_element_type=F32)


def feature_map(a):
    a = a.astype(F32)
    return jnp.where(a > 0.0, a + 1.0, jnp.exp(jnp.minimum(a, 0.0))).astype(BF16)


class Line:
    def __init__(self, me, device):
        self.me = me
        self.device = device

    def copy(self, src, dst, sems, send_at, recv_at, peer):
        return pltpu.make_async_remote_copy(
            src_ref=src,
            dst_ref=dst,
            send_sem=sems[0].at[send_at],
            recv_sem=sems[1].at[recv_at],
            device_id=self.device(peer),
            device_id_type=MESH,
        )

    def each(self, body):
        def run(i, carry):
            odd = i % 2
            k = SIDE // 2 + (i // 2) * (1 - 2 * odd) - odd
            body(lax.rem(self.me + k, SIDE))
            return carry

        lax.fori_loop(0, SIDE - 1, run, 0, unroll=True)

    def scatter(self, src, dst, sems):
        self.each(lambda t: self.copy(src.at[t], dst.at[self.me], sems, t, self.me, t).start())

    def spread(self, src, dst, sems):
        self.each(lambda t: self.copy(src, dst.at[self.me], sems, t, self.me, t).start())

    def wait_recv(self, dst, sems):
        self.each(lambda t: self.copy(dst.at[t], dst.at[t], sems, t, t, t).wait_recv())

    def wait_send(self, dst, sems):
        self.each(lambda t: self.copy(dst.at[t], dst.at[t], sems, t, t, t).wait_send())


class Scan:
    def __init__(self, zline, yline, bufs, sems, kind):
        self.z, self.y = zline, yline
        self.out, self.got, self.tot, self.back, self.result = bufs
        self.sz, self.sy, self.sb = sems[0:2], sems[2:4], sems[4:6]
        self.kind = kind

    def start(self):
        self.got[self.z.me] = self.out[self.z.me]
        self.z.scatter(self.out, self.got, self.sz)

    def start_part(self, low, high):
        for t in range(low, high):

            @pl.when(t == self.z.me)
            def _():
                self.got[t] = self.out[t]

            @pl.when(t != self.z.me)
            def _():
                at = self.z.me
                self.z.copy(self.out.at[t], self.got.at[at], self.sz, t, at, t).start()

    def middle(self):
        self.z.wait_recv(self.got, self.sz)
        if self.kind == "suffix":
            order = range(SIDE - 1, -1, -1)
        else:
            order = range(SIDE)
        total = None
        for at in order:
            if self.kind != "sum":
                self.back[at] = jnp.zeros_like(self.got[at]) if total is None else total
            total = self.got[at] if total is None else total + self.got[at]
        self.tot[self.y.me] = total
        self.y.spread(self.tot.at[self.y.me], self.tot, self.sy)

    def finish(self):
        self.y.wait_recv(self.tot, self.sy)
        base = jnp.zeros_like(self.tot[0])
        for at in range(SIDE):
            if self.kind == "sum":
                base = base + self.tot[at]
            else:
                counts = at < self.y.me if self.kind == "prefix" else at > self.y.me
                base = base + jnp.where(counts, self.tot[at], 0.0)
        if self.kind == "sum":
            self.result[self.z.me] = base
            self.z.spread(self.result.at[self.z.me], self.result, self.sb)
        else:
            for at in range(SIDE):
                self.back[at] = self.back[at] + base
            self.result[self.z.me] = self.back[self.z.me]
            self.z.scatter(self.back, self.result, self.sb)

    def wait(self):
        self.z.wait_recv(self.result, self.sb)

    def drain(self):
        self.z.wait_send(self.got, self.sz)
        self.y.wait_send(self.tot, self.sy)
        self.z.wait_send(self.result, self.sb)


class PairSum:
    def __init__(self, seq, mp, bufs, sems):
        self.seq = seq
        self.core, self.x = lax.rem(mp, 2), mp // 2
        self.part, self.other, self.row, self.total = bufs
        self.sem_a, self.sem_x, self.sem_b = sems

    def pair_copy(self, src, dst, sem):
        device = (self.seq, self.x * 2 + (1 - self.core))
        return pltpu.make_async_remote_copy(
            src_ref=src,
            dst_ref=dst,
            send_sem=sem.at[0],
            recv_sem=sem.at[1],
            device_id=device,
            device_id_type=MESH,
        )

    def x_copy(self, src, dst, send_at, recv_at, peer):
        return pltpu.make_async_remote_copy(
            src_ref=src,
            dst_ref=dst,
            send_sem=self.sem_x.at[send_at],
            recv_sem=self.sem_x.at[4 + recv_at],
            device_id=(self.seq, peer * 2 + self.core),
            device_id_type=MESH,
        )

    def peers(self):
        return [lax.rem(self.x + k, 4) for k in (2, 1, 3)]

    def start(self):
        self.first = self.pair_copy(self.part.at[1 - self.core], self.other, self.sem_a)
        self.first.start()

    def middle(self):
        self.first.wait_recv()
        self.row[self.x] = self.part[self.core] + self.other[...]
        mine = self.row.at[self.x]
        for t in self.peers():
            self.x_copy(mine, mine, t, self.x, t).start()

    def finish(self):
        for t in self.peers():
            self.x_copy(self.row.at[t], self.row.at[t], t, t, t).wait_recv()
        self.total[self.core] = (self.row[0] + self.row[1]) + (self.row[2] + self.row[3])
        mine = self.total.at[self.core]
        self.last = self.pair_copy(mine, mine, self.sem_b)
        self.last.start()

    def wait(self):
        other = self.total.at[1 - self.core]
        self.pair_copy(other, other, self.sem_b).wait_recv()
        return self.total[...].reshape(RANK, TOK)

    def drain(self):
        self.first.wait_send()
        for t in self.peers():
            self.x_copy(self.row.at[t], self.row.at[t], t, t, t).wait_send()
        self.last.wait_send()


def kernel(*refs):
    names = ("inputs", "queries", "keys", "values", "gain", "cot", "down", "up")
    names += ("mdown", "mup", "ndown", "nup")
    hbm = dict(zip(names, refs[:12]))
    scratch = list(refs[17:])

    def take(n):
        got = scratch[:n]
        del scratch[:n]
        return got

    x, q, k, v, gain, cot, down, up, mdown, mup, ndown, nup = take(12)
    vm = dict(zip(names, (x, q, k, v, gain, cot, down, up, mdown, mup, ndown, nup)))
    normed, o_down, o_mdown, o_up, o_mup = take(5)
    outs = list(zip((normed, o_down, o_mdown, o_up, o_mup), refs[12:17]))
    qf, kf, vmix, w, nearby, znear, grad, coef, low, near = take(10)
    kv_bufs, a_bufs, ub_bufs, gu_bufs, gd_bufs = take(5), take(5), take(5), take(5), take(5)
    p1_bufs, p2_bufs = take(4), take(4)
    load_sem, store_sem = take(2)

    def store(at):
        return pltpu.make_async_copy(*outs[at], store_sem.at[at])

    kv_sems, a_sems, ub_sems, gu_sems, gd_sems = take(6), take(6), take(6), take(6), take(6)
    p1_sems, p2_sems = take(3), take(3)

    seq, mp = lax.axis_index("seq"), lax.axis_index("mp")
    y, z = seq // SIDE, lax.rem(seq, SIDE)
    zline = Line(z, lambda t: (y * SIDE + t, mp))
    yline = Line(y, lambda t: (t * SIDE + z, mp))
    core, xpos = lax.rem(mp, 2), mp // 2

    kv = [
        Scan(zline, yline, [b.at[h] for b in kv_bufs], [m.at[h] for m in kv_sems], "prefix")
        for h in range(HEADS)
    ]
    pa = Scan(zline, yline, a_bufs, a_sems, "prefix")
    ub = Scan(zline, yline, ub_bufs, ub_sems, "suffix")
    gu = Scan(zline, yline, gu_bufs, gu_sems, "sum")
    gd = Scan(zline, yline, gd_bufs, gd_sems, "sum")
    p1 = PairSum(seq, mp, p1_bufs, p1_sems)
    p2 = PairSum(seq, mp, p2_bufs, p2_sems)

    barrier = pltpu.get_barrier_semaphore()
    signal = functools.partial(pl.semaphore_signal, barrier, inc=1, device_id_type=MESH)
    yline.each(lambda t: signal(device_id=yline.device(t)))
    zline.each(lambda t: signal(device_id=zline.device(t)))
    signal(device_id=(seq, xpos * 2 + (1 - core)))
    for t in p1.peers():
        signal(device_id=(seq, t * 2 + core))

    order = ("inputs", "down", "keys", "values", "queries", "up", "gain", "cot")
    order += ("mdown", "mup", "ndown", "nup")
    loads = {}
    for at, name in enumerate(order):
        loads[name] = pltpu.make_async_copy(hbm[name], vm[name], load_sem.at[at])
        loads[name].start()

    loads["inputs"].wait()
    loads["down"].wait()
    p1.part[...] = dot(down[...].astype(BF16), x[...], 1, 1).reshape(2, RANK // 2, TOK)

    def rows(i):
        return pl.ds(pl.multiple_of(i * CHUNK, CHUNK), CHUNK)

    def head(h):
        if isinstance(h, int):
            return slice(h * HEAD, (h + 1) * HEAD)
        return pl.ds(pl.multiple_of(h * HEAD, HEAD), HEAD)

    pl.semaphore_wait(barrier, 2 * (SIDE - 1) + 4)
    p1.start()

    loads["keys"].wait()

    def map_keys(i, c):
        kf[rows(i), :] = feature_map(k[rows(i), :])
        return c

    lax.fori_loop(0, CHUNKS, map_keys, 0)
    loads["values"].wait()

    def states(h):
        cols = slice(h * HEAD, (h + 1) * HEAD)
        kv_bufs[0][h] = dot(kf[:, cols], v[:, cols], 0, 0).reshape(SIDE, HEAD // SIDE, HEAD)
        kv[h].start()

    states(0)
    states(1)
    p1.middle()
    states(2)
    states(3)

    loads["queries"].wait()

    def map_queries(i, c):
        qf[rows(i), :] = feature_map(q[rows(i), :])
        return c

    lax.fori_loop(0, CHUNKS, map_queries, 0)

    def scores(h, c):
        for i in range(CHUNKS):
            at, width = i * CHUNK, (i + 1) * CHUNK
            s = dot(qf[at:width, head(h)], kf[:width, head(h)], 1, 1)
            t = lax.broadcasted_iota(jnp.int32, (CHUNK, width), 0) + at
            col = lax.broadcasted_iota(jnp.int32, (CHUNK, width), 1)
            w[h, at:width, :width] = jnp.where(t >= col, s, 0.0).astype(BF16)
        return c

    loads["up"].wait()
    p1.finish()
    kv[0].middle()
    kv[1].middle()
    inner = (p1.wait() * (1.0 / math.sqrt(D))).astype(BF16)
    coef[...] = inner
    share = dot(inner, kf[...], 1, 0)
    for h in range(HEADS):
        pa.out[2 * h : 2 * h + 2] = share[:, h * HEAD : (h + 1) * HEAD].reshape(2, RANK // 2, HEAD)
    pa.start()
    kv[2].middle()
    kv[3].middle()

    low[...] = jnp.transpose(inner.astype(F32)).astype(BF16)

    def mix(i, c):
        lifted = dot(low[rows(i), :], up[...].astype(BF16), 1, 0)
        vmix[rows(i), :] = (v[rows(i), :].astype(F32) + lifted * (1.0 / math.sqrt(RANK))).astype(BF16)
        return c

    lax.fori_loop(0, CHUNKS, mix, 0)
    lax.fori_loop(0, 1, scores, 0)
    pa.middle()
    kv[0].finish()
    kv[1].finish()
    lax.fori_loop(1, HEADS, scores, 0)

    def local(h, c):
        for i in range(CHUNKS):
            at, width = i * CHUNK, (i + 1) * CHUNK
            wc = w[h, at:width, :width]
            nearby[at:width, head(h)] = dot(wc, vmix[:width, head(h)], 1, 0)
            znear[h, at:width, :] = dot(wc, low[:width, :], 1, 0)
        return c

    kv[2].finish()
    kv[3].finish()
    pa.finish()
    lax.fori_loop(0, HEADS, local, 0)
    loads["gain"].wait()
    loads["cot"].wait()
    pa.wait()

    def attend(h, c):
        pre = pa.result[pl.ds(h * 2, 2)].reshape(RANK, HEAD).astype(BF16)
        uph = up[:, head(h)].astype(BF16)
        kv[h].wait()
        state = kv_bufs[4][h].reshape(HEAD, HEAD)
        state = (state + dot(pre, uph, 0, 0) * (1.0 / math.sqrt(RANK))).astype(BF16)
        g = gain[:, head(h)]
        for i in range(CHUNKS):
            r = slice(i * CHUNK, (i + 1) * CHUNK)
            summed = nearby[r, head(h)] + dot(qf[r, head(h)], state, 1, 0)
            gg = g * cot[r, head(h)].astype(F32)
            square = jnp.mean(summed * summed, axis=-1, keepdims=True)
            cross = jnp.mean(gg * summed, axis=-1, keepdims=True)
            inv = lax.rsqrt(square + epsilon)
            unit = summed * inv
            grad[r, head(h)] = (inv * gg - unit * (inv * inv * cross)).astype(BF16)
            normed[r, head(h)] = (g * unit).astype(BF16)
        return c

    def contract(h, c):
        uph = up[:, head(h)].astype(BF16)
        g = dot(uph, grad[:, head(h)], 1, 1).astype(BF16)
        p2_g[h] = g
        ub.out[pl.ds(h * 2, 2)] = dot(g, qf[:, head(h)], 1, 0).reshape(2, RANK // 2, HEAD)
        return c

    p2_g = scratch.pop(0)

    for h in range(HEADS):
        attend(h, 0)
    for h in range(HEADS):
        contract(h, 0)
        ub.start_part(2 * h, 2 * h + 2)
    store(0).start()
    def grad_up(h, c):
        pre = pa.result[pl.ds(h * 2, 2)].reshape(RANK, HEAD).astype(BF16)
        zsum = (znear[h] + dot(qf[:, head(h)], pre, 1, 1)).astype(BF16)
        gu.out[pl.ds(h * 2, 2)] = dot(zsum, grad[:, head(h)], 0, 0).reshape(2, RANK // 2, HEAD)
        return c

    lax.fori_loop(0, HEADS, grad_up, 0)
    near[...] = jnp.zeros_like(near)

    def back_near(h, c):
        for i in range(CHUNKS):
            at, width = i * CHUNK, (i + 1) * CHUNK
            near[:, at:width] += dot(p2_g[h, :, at:], w[h, at:, at:width], 1, 0)
        return c

    ub.middle()
    gu.start()
    lax.fori_loop(0, HEADS, back_near, 0)
    ub.finish()
    gu.middle()
    ub.wait()
    far = near[...]
    for h in range(HEADS):
        u = ub.result[2 * h : 2 * h + 2].reshape(RANK, HEAD).astype(BF16)
        far = far + dot(u, kf[:, h * HEAD : (h + 1) * HEAD], 1, 1)
    p2.part[...] = far.reshape(2, RANK // 2, TOK)
    p2.start()
    gu.finish()

    p2.middle()
    for name in ("mdown", "mup", "ndown", "nup"):
        loads[name].wait()
    p2.finish()
    gu.wait()
    up_total = gu.result[...].reshape(HEADS * RANK, HEAD)
    for h in range(HEADS):
        cols = slice(h * HEAD, (h + 1) * HEAD)
        total = up_total[h * RANK : (h + 1) * RANK] * (1.0 / math.sqrt(RANK))
        new = (1.0 - friction) * mup[:, cols] - step_rate * total + spread * nup[:, cols]
        o_mup[:, cols] = new
        o_up[:, cols] = up[:, cols] + new
    store(3).start()
    store(4).start()
    inner_grad = (p2.wait() * (1.0 / math.sqrt(RANK))).astype(BF16)
    share_down = dot(inner_grad, x[...], 1, 0) * (1.0 / math.sqrt(D))
    stacked = jnp.concatenate(
        [share_down[:, i * HEAD : (i + 1) * HEAD] for i in range(FEATS // HEAD)], axis=0
    )
    gd.out[...] = stacked.reshape(SIDE, RANK * FEATS // HEAD // SIDE, HEAD)
    gd.start()
    for h in range(HEADS):
        kv[h].drain()
    pa.drain()
    ub.drain()
    gd.middle()
    gu.drain()
    p1.drain()
    p2.drain()
    gd.finish()
    gd.wait()
    down_total = gd.result[...].reshape(RANK * FEATS // HEAD, HEAD)
    for i in range(FEATS // HEAD):
        cols = slice(i * HEAD, (i + 1) * HEAD)
        total = down_total[i * RANK : (i + 1) * RANK]
        new = (1.0 - friction) * mdown[:, cols] - step_rate * total + spread * ndown[:, cols]
        o_mdown[:, cols] = new
        o_down[:, cols] = down[:, cols] + new
    store(1).start()
    store(2).start()
    gd.drain()
    for at in range(len(outs)):
        store(at).wait()


def write_out(*refs):
    n = len(refs) // 2
    copies = [pltpu.make_async_copy(refs[i], refs[n + i], refs[-1].at[i]) for i in range(n)]
    for copy in copies:
        copy.start()
    for copy in copies:
        copy.wait()


def per_device(
    inputs,
    queries,
    key_rows,
    values,
    norm_gain,
    cotangent,
    adapter_down,
    adapter_up,
    moment_down,
    moment_up,
    noise_down,
    noise_up,
):
    args = (
        inputs,
        queries,
        key_rows,
        values,
        norm_gain.reshape(1, COLS),
        cotangent,
        adapter_down,
        adapter_up,
        moment_down,
        moment_up,
        noise_down,
        noise_up,
    )
    out_shape = (
        jax.ShapeDtypeStruct((TOK, COLS), BF16),
        jax.ShapeDtypeStruct((RANK, FEATS), F32),
        jax.ShapeDtypeStruct((RANK, FEATS), F32),
        jax.ShapeDtypeStruct((RANK, COLS), F32),
        jax.ShapeDtypeStruct((RANK, COLS), F32),
    )

    def scan_bufs(n):
        whole = pltpu.VMEM((SIDE, n, HEAD), F32)
        return [whole] * 5

    scratch = [pltpu.VMEM(a.shape, a.dtype) for a in args]
    scratch += [pltpu.VMEM(s.shape, s.dtype) for s in out_shape]
    scratch += [
        pltpu.VMEM((TOK, COLS), BF16),
        pltpu.VMEM((TOK, COLS), BF16),
        pltpu.VMEM((TOK, COLS), BF16),
        pltpu.VMEM((HEADS, TOK, TOK), BF16),
        pltpu.VMEM((TOK, COLS), F32),
        pltpu.VMEM((HEADS, TOK, RANK), F32),
        pltpu.VMEM((TOK, COLS), BF16),
        pltpu.VMEM((RANK, TOK), BF16),
        pltpu.VMEM((TOK, RANK), BF16),
        pltpu.VMEM((RANK, TOK), F32),
    ]
    scratch += [pltpu.VMEM((HEADS, SIDE, HEAD // SIDE, HEAD), F32)] * 5
    for n in (16, 16, 16, 24):
        scratch += scan_bufs(n)
    half = RANK // 2
    for _ in range(2):
        scratch += [
            pltpu.VMEM((2, half, TOK), F32),
            pltpu.VMEM((half, TOK), F32),
            pltpu.VMEM((4, half, TOK), F32),
            pltpu.VMEM((2, half, TOK), F32),
        ]
    sem = pltpu.SemaphoreType.DMA
    scratch += [sem((12,)), sem((5,))]
    scratch += [sem((HEADS, SIDE))] * 6
    scratch += [sem((SIDE,))] * 24
    scratch += [sem((2,)), sem((8,)), sem((2,))] * 2
    scratch += [pltpu.VMEM((HEADS, RANK, TOK), BF16)]
    anywhere = pl.BlockSpec(memory_space=pl.ANY)
    results = pl.pallas_call(
        kernel,
        out_shape=out_shape,
        in_specs=[anywhere] * len(args),
        out_specs=(anywhere,) * len(out_shape),
        scratch_shapes=scratch,
        compiler_params=pltpu.CompilerParams(
            collective_id=0, has_side_effects=True, vmem_limit_bytes=60 * 2**20
        ),
        name="fused_update",
    )(*args)
    return pl.pallas_call(
        write_out,
        out_shape=out_shape,
        in_specs=[pl.BlockSpec(memory_space=pltpu.VMEM)] * len(out_shape),
        out_specs=(anywhere,) * len(out_shape),
        scratch_shapes=[sem((len(out_shape),))],
        compiler_params=pltpu.CompilerParams(vmem_limit_bytes=60 * 2**20),
        name="write_out",
    )(*results)


def solution(mesh):
    return jax.shard_map(
        per_device,
        mesh=mesh,
        in_specs=(
            P("seq", "mp"),
            P("seq", "mp"),
            P("seq", "mp"),
            P("seq", "mp"),
            P("mp"),
            P("seq", "mp"),
            P(None, "mp"),
            P(None, "mp"),
            P(None, "mp"),
            P(None, "mp"),
            P(None, "mp"),
            P(None, "mp"),
        ),
        out_specs=(P("seq", "mp"), P(None, "mp"), P(None, "mp"), P(None, "mp"), P(None, "mp")),
        check_vma=False,
    )
```

```python
import functools
import math

import jax
import jax.numpy as jnp
from jax import lax
from jax.experimental import pallas as pl
from jax.experimental.pallas import tpu as pltpu
from jax.sharding import PartitionSpec as P

D = 6144
HEAD = 128
RANK = 32
STEP = 250
CYCLE = 1000
TOK = 640
HEADS = 4
COLS = HEADS * HEAD
FEATS = 768
CHUNK = 128
CHUNKS = TOK // CHUNK
SIDE = 8
MESH = pl.DeviceIdType.MESH

friction = 0.2
peak_rate = 0.03
epsilon = 1e-06
step_rate = peak_rate * (math.cos(math.pi * ((STEP - 1) % CYCLE) / CYCLE) + 1.0)
spread = math.sqrt(2.0 * friction * step_rate)

F32 = jnp.float32
BF16 = jnp.bfloat16


def dot(a, b, ca, cb):
    return lax.dot_general(a, b, (((ca,), (cb,)), ((), ())), preferred_element_type=F32)


def feature_map(a):
    a = a.astype(F32)
    return jnp.where(a > 0.0, a + 1.0, jnp.exp(jnp.minimum(a, 0.0))).astype(BF16)


class Line:
    def __init__(self, me, device):
        self.me = me
        self.device = device

    def copy(self, src, dst, sems, send_at, recv_at, peer):
        return pltpu.make_async_remote_copy(
            src_ref=src,
            dst_ref=dst,
            send_sem=sems[0].at[send_at],
            recv_sem=sems[1].at[recv_at],
            device_id=self.device(peer),
            device_id_type=MESH,
        )

    def each(self, body):
        def run(i, carry):
            odd = i % 2
            k = SIDE // 2 + (i // 2) * (1 - 2 * odd) - odd
            body(lax.rem(self.me + k, SIDE))
            return carry

        lax.fori_loop(0, SIDE - 1, run, 0, unroll=True)

    def scatter(self, src, dst, sems):
        self.each(lambda t: self.copy(src.at[t], dst.at[self.me], sems, t, self.me, t).start())

    def spread(self, src, dst, sems):
        self.each(lambda t: self.copy(src, dst.at[self.me], sems, t, self.me, t).start())

    def wait_recv(self, dst, sems):
        self.each(lambda t: self.copy(dst.at[t], dst.at[t], sems, t, t, t).wait_recv())

    def wait_send(self, dst, sems):
        self.each(lambda t: self.copy(dst.at[t], dst.at[t], sems, t, t, t).wait_send())


class Scan:
    def __init__(self, zline, yline, bufs, sems, kind):
        self.z, self.y = zline, yline
        self.out, self.got, self.tot, self.back, self.result = bufs
        self.sz, self.sy, self.sb = sems[0:2], sems[2:4], sems[4:6]
        self.kind = kind

    def start(self):
        self.got[self.z.me] = self.out[self.z.me]
        self.z.scatter(self.out, self.got, self.sz)

    def start_part(self, low, high):
        for t in range(low, high):

            @pl.when(t == self.z.me)
            def _():
                self.got[t] = self.out[t]

            @pl.when(t != self.z.me)
            def _():
                at = self.z.me
                self.z.copy(self.out.at[t], self.got.at[at], self.sz, t, at, t).start()

    def middle(self):
        self.z.wait_recv(self.got, self.sz)
        if self.kind == "suffix":
            order = range(SIDE - 1, -1, -1)
        else:
            order = range(SIDE)
        total = None
        for at in order:
            if self.kind != "sum":
                self.back[at] = jnp.zeros_like(self.got[at]) if total is None else total
            total = self.got[at] if total is None else total + self.got[at]
        self.tot[self.y.me] = total
        self.y.spread(self.tot.at[self.y.me], self.tot, self.sy)

    def finish(self):
        self.y.wait_recv(self.tot, self.sy)
        base = jnp.zeros_like(self.tot[0])
        for at in range(SIDE):
            if self.kind == "sum":
                base = base + self.tot[at]
            else:
                counts = at < self.y.me if self.kind == "prefix" else at > self.y.me
                base = base + jnp.where(counts, self.tot[at], 0.0)
        if self.kind == "sum":
            self.result[self.z.me] = base
            self.z.spread(self.result.at[self.z.me], self.result, self.sb)
        else:
            for at in range(SIDE):
                self.back[at] = self.back[at] + base
            self.result[self.z.me] = self.back[self.z.me]
            self.z.scatter(self.back, self.result, self.sb)

    def wait(self):
        self.z.wait_recv(self.result, self.sb)

    def drain(self):
        self.z.wait_send(self.got, self.sz)
        self.y.wait_send(self.tot, self.sy)
        self.z.wait_send(self.result, self.sb)


class PairSum:
    def __init__(self, seq, mp, bufs, sems):
        self.seq = seq
        self.core, self.x = lax.rem(mp, 2), mp // 2
        self.part, self.other, self.row, self.total = bufs
        self.sem_a, self.sem_x, self.sem_b = sems

    def pair_copy(self, src, dst, sem):
        device = (self.seq, self.x * 2 + (1 - self.core))
        return pltpu.make_async_remote_copy(
            src_ref=src,
            dst_ref=dst,
            send_sem=sem.at[0],
            recv_sem=sem.at[1],
            device_id=device,
            device_id_type=MESH,
        )

    def x_copy(self, src, dst, send_at, recv_at, peer):
        return pltpu.make_async_remote_copy(
            src_ref=src,
            dst_ref=dst,
            send_sem=self.sem_x.at[send_at],
            recv_sem=self.sem_x.at[4 + recv_at],
            device_id=(self.seq, peer * 2 + self.core),
            device_id_type=MESH,
        )

    def peers(self):
        return [lax.rem(self.x + k, 4) for k in (2, 1, 3)]

    def start(self):
        self.first = self.pair_copy(self.part.at[1 - self.core], self.other, self.sem_a)
        self.first.start()

    def middle(self):
        self.first.wait_recv()
        self.row[self.x] = self.part[self.core] + self.other[...]
        mine = self.row.at[self.x]
        for t in self.peers():
            self.x_copy(mine, mine, t, self.x, t).start()

    def finish(self):
        for t in self.peers():
            self.x_copy(self.row.at[t], self.row.at[t], t, t, t).wait_recv()
        self.total[self.core] = (self.row[0] + self.row[1]) + (self.row[2] + self.row[3])
        mine = self.total.at[self.core]
        self.last = self.pair_copy(mine, mine, self.sem_b)
        self.last.start()

    def wait(self):
        other = self.total.at[1 - self.core]
        self.pair_copy(other, other, self.sem_b).wait_recv()
        return self.total[...].reshape(RANK, TOK)

    def drain(self):
        self.first.wait_send()
        for t in self.peers():
            self.x_copy(self.row.at[t], self.row.at[t], t, t, t).wait_send()
        self.last.wait_send()


def kernel(*refs):
    names = ("inputs", "queries", "keys", "values", "gain", "cot", "down", "up")
    names += ("mdown", "mup", "ndown", "nup")
    hbm = dict(zip(names, refs[:12]))
    scratch = list(refs[17:])

    def take(n):
        got = scratch[:n]
        del scratch[:n]
        return got

    x, q, k, v, gain, cot, down, up, mdown, mup, ndown, nup = take(12)
    vm = dict(zip(names, (x, q, k, v, gain, cot, down, up, mdown, mup, ndown, nup)))
    normed, o_down, o_mdown, o_up, o_mup = take(5)
    outs = list(zip((normed, o_down, o_mdown, o_up, o_mup), refs[12:17]))
    qf, kf, vmix, w, nearby, znear, grad, coef, low, near = take(10)
    kv_bufs, a_bufs, ub_bufs, gu_bufs, gd_bufs = take(5), take(5), take(5), take(5), take(5)
    p1_bufs, p2_bufs = take(4), take(4)
    load_sem, store_sem = take(2)

    def store(at):
        return pltpu.make_async_copy(*outs[at], store_sem.at[at])

    kv_sems, a_sems, ub_sems, gu_sems, gd_sems = take(6), take(6), take(6), take(6), take(6)
    p1_sems, p2_sems = take(3), take(3)

    seq, mp = lax.axis_index("seq"), lax.axis_index("mp")
    y, z = seq // SIDE, lax.rem(seq, SIDE)
    zline = Line(z, lambda t: (y * SIDE + t, mp))
    yline = Line(y, lambda t: (t * SIDE + z, mp))
    core, xpos = lax.rem(mp, 2), mp // 2

    kv = [
        Scan(zline, yline, [b.at[h] for b in kv_bufs], [m.at[h] for m in kv_sems], "prefix")
        for h in range(HEADS)
    ]
    pa = Scan(zline, yline, a_bufs, a_sems, "prefix")
    ub = Scan(zline, yline, ub_bufs, ub_sems, "suffix")
    gu = Scan(zline, yline, gu_bufs, gu_sems, "sum")
    gd = Scan(zline, yline, gd_bufs, gd_sems, "sum")
    p1 = PairSum(seq, mp, p1_bufs, p1_sems)
    p2 = PairSum(seq, mp, p2_bufs, p2_sems)

    barrier = pltpu.get_barrier_semaphore()
    signal = functools.partial(pl.semaphore_signal, barrier, inc=1, device_id_type=MESH)
    yline.each(lambda t: signal(device_id=yline.device(t)))
    zline.each(lambda t: signal(device_id=zline.device(t)))
    signal(device_id=(seq, xpos * 2 + (1 - core)))
    for t in p1.peers():
        signal(device_id=(seq, t * 2 + core))

    order = ("down", "inputs", "keys", "values", "queries", "up", "gain", "cot")
    order += ("mdown", "mup", "ndown", "nup")
    loads = {}
    pieces = []
    for at, name in enumerate(order):
        if name == "inputs":
            for i in range(CHUNKS):
                part = pl.ds(i * CHUNK, CHUNK)
                piece = hbm[name].at[part], vm[name].at[part]
                pieces.append(pltpu.make_async_copy(*piece, load_sem.at[12 + i]))
                pieces[i].start()
            continue
        loads[name] = pltpu.make_async_copy(hbm[name], vm[name], load_sem.at[at])
        loads[name].start()

    loads["down"].wait()
    low_down = down[...].astype(BF16)
    for i in range(CHUNKS):
        pieces[i].wait()
        cols = slice(i * CHUNK, (i + 1) * CHUNK)
        share = dot(low_down, x[cols, :], 1, 1)
        p1.part[:, :, cols] = share.reshape(2, RANK // 2, CHUNK)

    def rows(i):
        return pl.ds(pl.multiple_of(i * CHUNK, CHUNK), CHUNK)

    def head(h):
        if isinstance(h, int):
            return slice(h * HEAD, (h + 1) * HEAD)
        return pl.ds(pl.multiple_of(h * HEAD, HEAD), HEAD)

    pl.semaphore_wait(barrier, 2 * (SIDE - 1) + 4)
    p1.start()

    loads["keys"].wait()

    def map_keys(i, c):
        kf[rows(i), :] = feature_map(k[rows(i), :])
        return c

    lax.fori_loop(0, CHUNKS, map_keys, 0)
    p1.middle()
    loads["values"].wait()

    def states(h):
        cols = slice(h * HEAD, (h + 1) * HEAD)
        kv_bufs[0][h] = dot(kf[:, cols], v[:, cols], 0, 0).reshape(SIDE, HEAD // SIDE, HEAD)
        kv[h].start()

    states(0)
    states(1)
    states(2)
    states(3)

    loads["queries"].wait()

    def map_queries(i, c):
        qf[rows(i), :] = feature_map(q[rows(i), :])
        return c

    lax.fori_loop(0, CHUNKS, map_queries, 0)

    def scores(h, c):
        for i in range(CHUNKS):
            at, width = i * CHUNK, (i + 1) * CHUNK
            s = dot(qf[at:width, head(h)], kf[:width, head(h)], 1, 1)
            t = lax.broadcasted_iota(jnp.int32, (CHUNK, width), 0) + at
            col = lax.broadcasted_iota(jnp.int32, (CHUNK, width), 1)
            w[h, at:width, :width] = jnp.where(t >= col, s, 0.0).astype(BF16)
        return c

    lax.fori_loop(0, 1, scores, 0)
    loads["up"].wait()
    p1.finish()
    kv[0].middle()
    kv[1].middle()
    inner = (p1.wait() * (1.0 / math.sqrt(D))).astype(BF16)
    coef[...] = inner
    share = dot(inner, kf[...], 1, 0)
    for h in range(HEADS):
        pa.out[2 * h : 2 * h + 2] = share[:, h * HEAD : (h + 1) * HEAD].reshape(2, RANK // 2, HEAD)
    pa.start()
    kv[2].middle()
    kv[3].middle()

    low[...] = jnp.transpose(inner.astype(F32)).astype(BF16)

    def mix(i, c):
        lifted = dot(low[rows(i), :], up[...].astype(BF16), 1, 0)
        vmix[rows(i), :] = (v[rows(i), :].astype(F32) + lifted * (1.0 / math.sqrt(RANK))).astype(BF16)
        return c

    lax.fori_loop(0, CHUNKS, mix, 0)
    kv[0].finish()
    kv[1].finish()
    pa.middle()
    kv[2].finish()
    kv[3].finish()
    lax.fori_loop(1, HEADS, scores, 0)

    def local(h, c):
        for i in range(CHUNKS):
            at, width = i * CHUNK, (i + 1) * CHUNK
            wc = w[h, at:width, :width]
            nearby[at:width, head(h)] = dot(wc, vmix[:width, head(h)], 1, 0)
            znear[h, at:width, :] = dot(wc, low[:width, :], 1, 0)
        return c

    pa.finish()
    lax.fori_loop(0, HEADS, local, 0)
    loads["gain"].wait()
    loads["cot"].wait()
    pa.wait()

    def attend(h, c):
        pre = pa.result[pl.ds(h * 2, 2)].reshape(RANK, HEAD).astype(BF16)
        uph = up[:, head(h)].astype(BF16)
        kv[h].wait()
        state = kv_bufs[4][h].reshape(HEAD, HEAD)
        state = (state + dot(pre, uph, 0, 0) * (1.0 / math.sqrt(RANK))).astype(BF16)
        g = gain[:, head(h)]
        for i in range(CHUNKS):
            r = slice(i * CHUNK, (i + 1) * CHUNK)
            summed = nearby[r, head(h)] + dot(qf[r, head(h)], state, 1, 0)
            gg = g * cot[r, head(h)].astype(F32)
            square = jnp.mean(summed * summed, axis=-1, keepdims=True)
            cross = jnp.mean(gg * summed, axis=-1, keepdims=True)
            inv = lax.rsqrt(square + epsilon)
            unit = summed * inv
            grad[r, head(h)] = (inv * gg - unit * (inv * inv * cross)).astype(BF16)
            normed[r, head(h)] = (g * unit).astype(BF16)
        return c

    def contract(h, c):
        uph = up[:, head(h)].astype(BF16)
        g = dot(uph, grad[:, head(h)], 1, 1).astype(BF16)
        p2_g[h] = g
        ub.out[pl.ds(h * 2, 2)] = dot(g, qf[:, head(h)], 1, 0).reshape(2, RANK // 2, HEAD)
        return c

    p2_g = scratch.pop(0)

    for h in range(HEADS):
        attend(h, 0)
    for h in range(HEADS):
        contract(h, 0)
    ub.start()
    store(0).start()
    def grad_up(h, c):
        pre = pa.result[pl.ds(h * 2, 2)].reshape(RANK, HEAD).astype(BF16)
        zsum = (znear[h] + dot(qf[:, head(h)], pre, 1, 1)).astype(BF16)
        gu.out[pl.ds(h * 2, 2)] = dot(zsum, grad[:, head(h)], 0, 0).reshape(2, RANK // 2, HEAD)
        return c

    lax.fori_loop(0, HEADS, grad_up, 0)
    near[...] = jnp.zeros_like(near)

    def back_near(h, c):
        for i in range(CHUNKS):
            at, width = i * CHUNK, (i + 1) * CHUNK
            near[:, at:width] += dot(p2_g[h, :, at:], w[h, at:, at:width], 1, 0)
        return c

    ub.middle()
    gu.start()
    lax.fori_loop(0, HEADS, back_near, 0)
    ub.finish()
    gu.middle()
    for h in range(HEADS):
        kv[h].drain()
    pa.drain()
    p1.drain()
    ub.wait()
    far = near[...]
    for h in range(HEADS):
        u = ub.result[2 * h : 2 * h + 2].reshape(RANK, HEAD).astype(BF16)
        far = far + dot(u, kf[:, h * HEAD : (h + 1) * HEAD], 1, 1)
    p2.part[...] = far.reshape(2, RANK // 2, TOK)
    p2.start()
    gu.finish()

    p2.middle()
    ub.drain()
    for name in ("mdown", "mup", "ndown", "nup"):
        loads[name].wait()
    p2.finish()
    inner_grad = (p2.wait() * (1.0 / math.sqrt(RANK))).astype(BF16)
    share_down = dot(inner_grad, x[...], 1, 0) * (1.0 / math.sqrt(D))
    stacked = jnp.concatenate(
        [share_down[:, i * HEAD : (i + 1) * HEAD] for i in range(FEATS // HEAD)], axis=0
    )
    gd.out[...] = stacked.reshape(SIDE, RANK * FEATS // HEAD // SIDE, HEAD)
    gd.start()
    gu.wait()
    up_total = gu.result[...].reshape(HEADS * RANK, HEAD)
    for h in range(HEADS):
        cols = slice(h * HEAD, (h + 1) * HEAD)
        total = up_total[h * RANK : (h + 1) * RANK] * (1.0 / math.sqrt(RANK))
        new = (1.0 - friction) * mup[:, cols] - step_rate * total + spread * nup[:, cols]
        o_mup[:, cols] = new
        o_up[:, cols] = up[:, cols] + new
    store(3).start()
    store(4).start()
    gd.middle()
    gu.drain()
    p2.drain()
    gd.finish()
    gd.wait()
    down_total = gd.result[...].reshape(RANK * FEATS // HEAD, HEAD)
    for i in range(FEATS // HEAD):
        cols = slice(i * HEAD, (i + 1) * HEAD)
        total = down_total[i * RANK : (i + 1) * RANK]
        new = (1.0 - friction) * mdown[:, cols] - step_rate * total + spread * ndown[:, cols]
        o_mdown[:, cols] = new
        o_down[:, cols] = down[:, cols] + new
    store(1).start()
    store(2).start()
    gd.drain()
    for at in range(len(outs)):
        store(at).wait()


def write_out(*refs):
    n = len(refs) // 3
    pieces = []
    for at in range(n):
        src, dst, held = refs[at], refs[n + at], refs[2 * n + at]
        steps = 4 if at == 0 else 1
        rows = src.shape[0] // steps
        for k in range(steps):
            part = pl.ds(k * rows, rows)
            pieces.append((src.at[part], held.at[part], dst.at[part]))
    sem = refs[-1]
    reads = [pltpu.make_async_copy(p[0], p[1], sem.at[0, i]) for i, p in enumerate(pieces)]
    writes = [pltpu.make_async_copy(p[1], p[2], sem.at[1, i]) for i, p in enumerate(pieces)]
    for copy in reads:
        copy.start()
    for read, write in zip(reads, writes):
        read.wait()
        write.start()
    for copy in writes:
        copy.wait()


def per_device(
    inputs,
    queries,
    key_rows,
    values,
    norm_gain,
    cotangent,
    adapter_down,
    adapter_up,
    moment_down,
    moment_up,
    noise_down,
    noise_up,
):
    args = (
        inputs,
        queries,
        key_rows,
        values,
        norm_gain.reshape(1, COLS),
        cotangent,
        adapter_down,
        adapter_up,
        moment_down,
        moment_up,
        noise_down,
        noise_up,
    )
    out_shape = (
        jax.ShapeDtypeStruct((TOK, COLS), BF16),
        jax.ShapeDtypeStruct((RANK, FEATS), F32),
        jax.ShapeDtypeStruct((RANK, FEATS), F32),
        jax.ShapeDtypeStruct((RANK, COLS), F32),
        jax.ShapeDtypeStruct((RANK, COLS), F32),
    )

    def scan_bufs(n):
        whole = pltpu.VMEM((SIDE, n, HEAD), F32)
        return [whole] * 5

    scratch = [pltpu.VMEM(a.shape, a.dtype) for a in args]
    scratch += [pltpu.VMEM(s.shape, s.dtype) for s in out_shape]
    scratch += [
        pltpu.VMEM((TOK, COLS), BF16),
        pltpu.VMEM((TOK, COLS), BF16),
        pltpu.VMEM((TOK, COLS), BF16),
        pltpu.VMEM((HEADS, TOK, TOK), BF16),
        pltpu.VMEM((TOK, COLS), F32),
        pltpu.VMEM((HEADS, TOK, RANK), F32),
        pltpu.VMEM((TOK, COLS), BF16),
        pltpu.VMEM((RANK, TOK), BF16),
        pltpu.VMEM((TOK, RANK), BF16),
        pltpu.VMEM((RANK, TOK), F32),
    ]
    scratch += [pltpu.VMEM((HEADS, SIDE, HEAD // SIDE, HEAD), F32)] * 5
    for n in (16, 16, 16, 24):
        scratch += scan_bufs(n)
    half = RANK // 2
    for _ in range(2):
        scratch += [
            pltpu.VMEM((2, half, TOK), F32),
            pltpu.VMEM((half, TOK), F32),
            pltpu.VMEM((4, half, TOK), F32),
            pltpu.VMEM((2, half, TOK), F32),
        ]
    sem = pltpu.SemaphoreType.DMA
    scratch += [sem((12 + CHUNKS,)), sem((5,))]
    scratch += [sem((HEADS, SIDE))] * 6
    scratch += [sem((SIDE,))] * 24
    scratch += [sem((2,)), sem((8,)), sem((2,))] * 2
    scratch += [pltpu.VMEM((HEADS, RANK, TOK), BF16)]
    anywhere = pl.BlockSpec(memory_space=pl.ANY)
    results = pl.pallas_call(
        kernel,
        out_shape=out_shape,
        in_specs=[anywhere] * len(args),
        out_specs=(anywhere,) * len(out_shape),
        scratch_shapes=scratch,
        compiler_params=pltpu.CompilerParams(
            collective_id=0, has_side_effects=True, vmem_limit_bytes=60 * 2**20
        ),
        name="fused_update",
    )(*args)
    return pl.pallas_call(
        write_out,
        out_shape=out_shape,
        in_specs=[anywhere] * len(out_shape),
        out_specs=(anywhere,) * len(out_shape),
        scratch_shapes=[pltpu.VMEM(s.shape, s.dtype) for s in out_shape] + [sem((2, 8))],
        compiler_params=pltpu.CompilerParams(vmem_limit_bytes=60 * 2**20),
        name="write_out",
    )(*results)


def solution(mesh):
    return jax.shard_map(
        per_device,
        mesh=mesh,
        in_specs=(
            P("seq", "mp"),
            P("seq", "mp"),
            P("seq", "mp"),
            P("seq", "mp"),
            P("mp"),
            P("seq", "mp"),
            P(None, "mp"),
            P(None, "mp"),
            P(None, "mp"),
            P(None, "mp"),
            P(None, "mp"),
            P(None, "mp"),
        ),
        out_specs=(P("seq", "mp"), P(None, "mp"), P(None, "mp"), P(None, "mp"), P(None, "mp")),
        check_vma=False,
    )
```

```python
import functools
import math

import jax
import jax.numpy as jnp
from jax import lax
from jax.experimental import pallas as pl
from jax.experimental.pallas import tpu as pltpu
from jax.sharding import PartitionSpec as P

D = 6144
HEAD = 128
RANK = 32
STEP = 250
CYCLE = 1000
TOK = 640
HEADS = 4
COLS = HEADS * HEAD
FEATS = 768
CHUNK = 128
CHUNKS = TOK // CHUNK
SIDE = 8
MESH = pl.DeviceIdType.MESH

friction = 0.2
peak_rate = 0.03
epsilon = 1e-06
step_rate = peak_rate * (math.cos(math.pi * ((STEP - 1) % CYCLE) / CYCLE) + 1.0)
spread = math.sqrt(2.0 * friction * step_rate)

F32 = jnp.float32
BF16 = jnp.bfloat16


def dot(a, b, ca, cb):
    return lax.dot_general(a, b, (((ca,), (cb,)), ((), ())), preferred_element_type=F32)


def feature_map(a):
    a = a.astype(F32)
    return jnp.where(a > 0.0, a + 1.0, jnp.exp(jnp.minimum(a, 0.0))).astype(BF16)


class Line:
    def __init__(self, me, device):
        self.me = me
        self.device = device

    def copy(self, src, dst, sems, send_at, recv_at, peer):
        return pltpu.make_async_remote_copy(
            src_ref=src,
            dst_ref=dst,
            send_sem=sems[0].at[send_at],
            recv_sem=sems[1].at[recv_at],
            device_id=self.device(peer),
            device_id_type=MESH,
        )

    def each(self, body):
        def run(i, carry):
            odd = i % 2
            k = SIDE // 2 + (i // 2) * (1 - 2 * odd) - odd
            body(lax.rem(self.me + k, SIDE))
            return carry

        lax.fori_loop(0, SIDE - 1, run, 0, unroll=True)

    def scatter(self, src, dst, sems):
        self.each(lambda t: self.copy(src.at[t], dst.at[self.me], sems, t, self.me, t).start())

    def spread(self, src, dst, sems):
        self.each(lambda t: self.copy(src, dst.at[self.me], sems, t, self.me, t).start())

    def wait_recv(self, dst, sems):
        self.each(lambda t: self.copy(dst.at[t], dst.at[t], sems, t, t, t).wait_recv())

    def wait_send(self, dst, sems):
        self.each(lambda t: self.copy(dst.at[t], dst.at[t], sems, t, t, t).wait_send())


class Scan:
    def __init__(self, zline, yline, bufs, sems, kind):
        self.z, self.y = zline, yline
        self.out, self.got, self.tot, self.back, self.result = bufs
        self.sz, self.sy, self.sb = sems[0:2], sems[2:4], sems[4:6]
        self.kind = kind

    def start(self):
        self.got[self.z.me] = self.out[self.z.me]
        self.z.scatter(self.out, self.got, self.sz)

    def start_part(self, low, high):
        for t in range(low, high):

            @pl.when(t == self.z.me)
            def _():
                self.got[t] = self.out[t]

            @pl.when(t != self.z.me)
            def _():
                at = self.z.me
                self.z.copy(self.out.at[t], self.got.at[at], self.sz, t, at, t).start()

    def middle(self):
        self.z.wait_recv(self.got, self.sz)
        if self.kind == "suffix":
            order = range(SIDE - 1, -1, -1)
        else:
            order = range(SIDE)
        total = None
        for at in order:
            if self.kind != "sum":
                self.back[at] = jnp.zeros_like(self.got[at]) if total is None else total
            total = self.got[at] if total is None else total + self.got[at]
        self.tot[self.y.me] = total
        self.y.spread(self.tot.at[self.y.me], self.tot, self.sy)

    def finish(self):
        self.y.wait_recv(self.tot, self.sy)
        base = jnp.zeros_like(self.tot[0])
        for at in range(SIDE):
            if self.kind == "sum":
                base = base + self.tot[at]
            else:
                counts = at < self.y.me if self.kind == "prefix" else at > self.y.me
                base = base + jnp.where(counts, self.tot[at], 0.0)
        if self.kind == "sum":
            self.result[self.z.me] = base
            self.z.spread(self.result.at[self.z.me], self.result, self.sb)
        else:
            for at in range(SIDE):
                self.back[at] = self.back[at] + base
            self.result[self.z.me] = self.back[self.z.me]
            self.z.scatter(self.back, self.result, self.sb)

    def wait(self):
        self.z.wait_recv(self.result, self.sb)

    def drain(self):
        self.z.wait_send(self.got, self.sz)
        self.y.wait_send(self.tot, self.sy)
        self.z.wait_send(self.result, self.sb)


class PairSum:
    def __init__(self, seq, mp, bufs, sems):
        self.seq = seq
        self.core, self.x = lax.rem(mp, 2), mp // 2
        self.part, self.other, self.row, self.total = bufs
        self.sem_a, self.sem_x, self.sem_b = sems

    def pair_copy(self, src, dst, sem):
        device = (self.seq, self.x * 2 + (1 - self.core))
        return pltpu.make_async_remote_copy(
            src_ref=src,
            dst_ref=dst,
            send_sem=sem.at[0],
            recv_sem=sem.at[1],
            device_id=device,
            device_id_type=MESH,
        )

    def x_copy(self, src, dst, send_at, recv_at, peer):
        return pltpu.make_async_remote_copy(
            src_ref=src,
            dst_ref=dst,
            send_sem=self.sem_x.at[send_at],
            recv_sem=self.sem_x.at[4 + recv_at],
            device_id=(self.seq, peer * 2 + self.core),
            device_id_type=MESH,
        )

    def peers(self):
        return [lax.rem(self.x + k, 4) for k in (2, 1, 3)]

    def start(self):
        self.first = self.pair_copy(self.part.at[1 - self.core], self.other, self.sem_a)
        self.first.start()

    def middle(self):
        self.first.wait_recv()
        self.row[self.x] = self.part[self.core] + self.other[...]
        mine = self.row.at[self.x]
        for t in self.peers():
            self.x_copy(mine, mine, t, self.x, t).start()

    def finish(self):
        for t in self.peers():
            self.x_copy(self.row.at[t], self.row.at[t], t, t, t).wait_recv()
        self.total[self.core] = (self.row[0] + self.row[1]) + (self.row[2] + self.row[3])
        mine = self.total.at[self.core]
        self.last = self.pair_copy(mine, mine, self.sem_b)
        self.last.start()

    def wait(self):
        other = self.total.at[1 - self.core]
        self.pair_copy(other, other, self.sem_b).wait_recv()
        return self.total[...].reshape(RANK, TOK)

    def drain(self):
        self.first.wait_send()
        for t in self.peers():
            self.x_copy(self.row.at[t], self.row.at[t], t, t, t).wait_send()
        self.last.wait_send()


def kernel(*refs):
    names = ("inputs", "queries", "keys", "values", "gain", "cot", "down", "up")
    names += ("mdown", "mup", "ndown", "nup")
    hbm = dict(zip(names, refs[:12]))
    scratch = list(refs[17:])

    def take(n):
        got = scratch[:n]
        del scratch[:n]
        return got

    x, q, k, v, gain, cot, down, up, mdown, mup, ndown, nup = take(12)
    vm = dict(zip(names, (x, q, k, v, gain, cot, down, up, mdown, mup, ndown, nup)))
    normed, o_down, o_mdown, o_up, o_mup = take(5)
    outs = list(zip((normed, o_down, o_mdown, o_up, o_mup), refs[12:17]))
    qf, kf, vmix, w, nearby, znear, grad, coef, low, near = take(10)
    kv_bufs, a_bufs, ub_bufs, gu_bufs, gd_bufs = take(5), take(5), take(5), take(5), take(5)
    p1_bufs, p2_bufs = take(4), take(4)
    load_sem, store_sem = take(2)

    def store(at):
        return pltpu.make_async_copy(*outs[at], store_sem.at[at])

    kv_sems, a_sems, ub_sems, gu_sems, gd_sems = take(6), take(6), take(6), take(6), take(6)
    p1_sems, p2_sems = take(3), take(3)

    seq, mp = lax.axis_index("seq"), lax.axis_index("mp")
    y, z = seq // SIDE, lax.rem(seq, SIDE)
    zline = Line(z, lambda t: (y * SIDE + t, mp))
    yline = Line(y, lambda t: (t * SIDE + z, mp))
    core, xpos = lax.rem(mp, 2), mp // 2

    kv = [
        Scan(zline, yline, [b.at[h] for b in kv_bufs], [m.at[h] for m in kv_sems], "prefix")
        for h in range(HEADS)
    ]
    pa = Scan(zline, yline, a_bufs, a_sems, "prefix")
    ub = Scan(zline, yline, ub_bufs, ub_sems, "suffix")
    gu = Scan(zline, yline, gu_bufs, gu_sems, "sum")
    gd = Scan(zline, yline, gd_bufs, gd_sems, "sum")
    p1 = PairSum(seq, mp, p1_bufs, p1_sems)
    p2 = PairSum(seq, mp, p2_bufs, p2_sems)

    barrier = pltpu.get_barrier_semaphore()
    signal = functools.partial(pl.semaphore_signal, barrier, inc=1, device_id_type=MESH)
    yline.each(lambda t: signal(device_id=yline.device(t)))
    zline.each(lambda t: signal(device_id=zline.device(t)))
    signal(device_id=(seq, xpos * 2 + (1 - core)))
    for t in p1.peers():
        signal(device_id=(seq, t * 2 + core))

    order = ("down", "inputs", "keys", "values", "queries", "up", "gain", "cot")
    order += ("mdown", "mup", "ndown", "nup")
    loads = {}
    pieces = []
    for at, name in enumerate(order):
        if name == "inputs":
            for i in range(CHUNKS):
                part = pl.ds(i * CHUNK, CHUNK)
                piece = hbm[name].at[part], vm[name].at[part]
                pieces.append(pltpu.make_async_copy(*piece, load_sem.at[12 + i]))
                pieces[i].start()
            continue
        loads[name] = pltpu.make_async_copy(hbm[name], vm[name], load_sem.at[at])
        loads[name].start()

    loads["down"].wait()
    low_down = down[...].astype(BF16)
    for i in range(CHUNKS):
        pieces[i].wait()
        cols = slice(i * CHUNK, (i + 1) * CHUNK)
        share = dot(low_down, x[cols, :], 1, 1)
        p1.part[:, :, cols] = share.reshape(2, RANK // 2, CHUNK)

    def rows(i):
        return pl.ds(pl.multiple_of(i * CHUNK, CHUNK), CHUNK)

    def head(h):
        if isinstance(h, int):
            return slice(h * HEAD, (h + 1) * HEAD)
        return pl.ds(pl.multiple_of(h * HEAD, HEAD), HEAD)

    pl.semaphore_wait(barrier, 2 * (SIDE - 1) + 4)
    p1.start()

    loads["keys"].wait()

    def map_keys(i, c):
        kf[rows(i), :] = feature_map(k[rows(i), :])
        return c

    lax.fori_loop(0, CHUNKS, map_keys, 0)
    p1.middle()
    loads["values"].wait()

    def states(h):
        cols = slice(h * HEAD, (h + 1) * HEAD)
        kv_bufs[0][h] = dot(kf[:, cols], v[:, cols], 0, 0).reshape(SIDE, HEAD // SIDE, HEAD)
        kv[h].start()

    states(0)
    states(1)
    states(2)
    states(3)

    loads["queries"].wait()

    def map_queries(i, c):
        qf[rows(i), :] = feature_map(q[rows(i), :])
        return c

    lax.fori_loop(0, CHUNKS, map_queries, 0)

    def scores(h, c):
        for i in range(CHUNKS):
            at, width = i * CHUNK, (i + 1) * CHUNK
            s = dot(qf[at:width, head(h)], kf[:width, head(h)], 1, 1)
            t = lax.broadcasted_iota(jnp.int32, (CHUNK, width), 0) + at
            col = lax.broadcasted_iota(jnp.int32, (CHUNK, width), 1)
            w[h, at:width, :width] = jnp.where(t >= col, s, 0.0).astype(BF16)
        return c

    loads["up"].wait()
    p1.finish()
    kv[0].middle()
    inner = (p1.wait() * (1.0 / math.sqrt(D))).astype(BF16)
    coef[...] = inner
    share = dot(inner, kf[...], 1, 0)
    for h in range(HEADS):
        pa.out[2 * h : 2 * h + 2] = share[:, h * HEAD : (h + 1) * HEAD].reshape(2, RANK // 2, HEAD)
    pa.start()
    kv[1].middle()
    kv[2].middle()
    kv[3].middle()

    low[...] = jnp.transpose(inner.astype(F32)).astype(BF16)

    def mix(i, c):
        lifted = dot(low[rows(i), :], up[...].astype(BF16), 1, 0)
        vmix[rows(i), :] = (v[rows(i), :].astype(F32) + lifted * (1.0 / math.sqrt(RANK))).astype(BF16)
        return c

    lax.fori_loop(0, CHUNKS, mix, 0)
    kv[0].finish()
    kv[1].finish()
    pa.middle()
    kv[2].finish()
    kv[3].finish()
    lax.fori_loop(0, HEADS, scores, 0)

    def local(h, c):
        for i in range(CHUNKS):
            at, width = i * CHUNK, (i + 1) * CHUNK
            wc = w[h, at:width, :width]
            nearby[at:width, head(h)] = dot(wc, vmix[:width, head(h)], 1, 0)
            znear[h, at:width, :] = dot(wc, low[:width, :], 1, 0)
        return c

    pa.finish()
    lax.fori_loop(0, HEADS, local, 0)
    loads["gain"].wait()
    loads["cot"].wait()
    pa.wait()

    def attend(h, c):
        pre = pa.result[pl.ds(h * 2, 2)].reshape(RANK, HEAD).astype(BF16)
        uph = up[:, head(h)].astype(BF16)
        kv[h].wait()
        state = kv_bufs[4][h].reshape(HEAD, HEAD)
        state = (state + dot(pre, uph, 0, 0) * (1.0 / math.sqrt(RANK))).astype(BF16)
        g = gain[:, head(h)]
        for i in range(CHUNKS):
            r = slice(i * CHUNK, (i + 1) * CHUNK)
            summed = nearby[r, head(h)] + dot(qf[r, head(h)], state, 1, 0)
            gg = g * cot[r, head(h)].astype(F32)
            square = jnp.mean(summed * summed, axis=-1, keepdims=True)
            cross = jnp.mean(gg * summed, axis=-1, keepdims=True)
            inv = lax.rsqrt(square + epsilon)
            unit = summed * inv
            grad[r, head(h)] = (inv * gg - unit * (inv * inv * cross)).astype(BF16)
            normed[r, head(h)] = (g * unit).astype(BF16)
        return c

    def contract(h, c):
        uph = up[:, head(h)].astype(BF16)
        g = dot(uph, grad[:, head(h)], 1, 1).astype(BF16)
        p2_g[h] = g
        ub.out[pl.ds(h * 2, 2)] = dot(g, qf[:, head(h)], 1, 0).reshape(2, RANK // 2, HEAD)
        return c

    p2_g = scratch.pop(0)

    for h in range(HEADS):
        attend(h, 0)
    for h in range(HEADS):
        contract(h, 0)
    ub.start()
    store(0).start()
    def grad_up(h, c):
        pre = pa.result[pl.ds(h * 2, 2)].reshape(RANK, HEAD).astype(BF16)
        zsum = (znear[h] + dot(qf[:, head(h)], pre, 1, 1)).astype(BF16)
        gu.out[pl.ds(h * 2, 2)] = dot(zsum, grad[:, head(h)], 0, 0).reshape(2, RANK // 2, HEAD)
        return c

    lax.fori_loop(0, HEADS, grad_up, 0)
    near[...] = jnp.zeros_like(near)

    def back_near(h, c):
        for i in range(CHUNKS):
            at, width = i * CHUNK, (i + 1) * CHUNK
            near[:, at:width] += dot(p2_g[h, :, at:], w[h, at:, at:width], 1, 0)
        return c

    ub.middle()
    gu.start()
    lax.fori_loop(0, HEADS, back_near, 0)
    ub.finish()
    gu.middle()
    for h in range(HEADS):
        kv[h].drain()
    pa.drain()
    p1.drain()
    ub.wait()
    far = near[...]
    for h in range(HEADS):
        u = ub.result[2 * h : 2 * h + 2].reshape(RANK, HEAD).astype(BF16)
        far = far + dot(u, kf[:, h * HEAD : (h + 1) * HEAD], 1, 1)
    p2.part[...] = far.reshape(2, RANK // 2, TOK)
    p2.start()
    p2.middle()
    gu.finish()
    ub.drain()
    for name in ("mdown", "mup", "ndown", "nup"):
        loads[name].wait()
    p2.finish()
    inner_grad = (p2.wait() * (1.0 / math.sqrt(RANK))).astype(BF16)
    share_down = dot(inner_grad, x[...], 1, 0) * (1.0 / math.sqrt(D))
    stacked = jnp.concatenate(
        [share_down[:, i * HEAD : (i + 1) * HEAD] for i in range(FEATS // HEAD)], axis=0
    )
    gd.out[...] = stacked.reshape(SIDE, RANK * FEATS // HEAD // SIDE, HEAD)
    gd.start()
    gu.wait()
    up_total = gu.result[...].reshape(HEADS * RANK, HEAD)
    for h in range(HEADS):
        cols = slice(h * HEAD, (h + 1) * HEAD)
        total = up_total[h * RANK : (h + 1) * RANK] * (1.0 / math.sqrt(RANK))
        new = (1.0 - friction) * mup[:, cols] - step_rate * total + spread * nup[:, cols]
        o_mup[:, cols] = new
        o_up[:, cols] = up[:, cols] + new
    store(3).start()
    store(4).start()
    gd.middle()
    gu.drain()
    p2.drain()
    gd.finish()
    gd.wait()
    down_total = gd.result[...].reshape(RANK * FEATS // HEAD, HEAD)
    for i in range(FEATS // HEAD):
        cols = slice(i * HEAD, (i + 1) * HEAD)
        total = down_total[i * RANK : (i + 1) * RANK]
        new = (1.0 - friction) * mdown[:, cols] - step_rate * total + spread * ndown[:, cols]
        o_mdown[:, cols] = new
        o_down[:, cols] = down[:, cols] + new
    store(1).start()
    store(2).start()
    gd.drain()
    for at in range(len(outs)):
        store(at).wait()


def write_out(*refs):
    n = len(refs) // 3
    pieces = []
    for at in range(n):
        src, dst, held = refs[at], refs[n + at], refs[2 * n + at]
        steps = 4 if at == 0 else 1
        rows = src.shape[0] // steps
        for k in range(steps):
            part = pl.ds(k * rows, rows)
            pieces.append((src.at[part], held.at[part], dst.at[part]))
    sem = refs[-1]
    reads = [pltpu.make_async_copy(p[0], p[1], sem.at[0, i]) for i, p in enumerate(pieces)]
    writes = [pltpu.make_async_copy(p[1], p[2], sem.at[1, i]) for i, p in enumerate(pieces)]
    for copy in reads:
        copy.start()
    for read, write in zip(reads, writes):
        read.wait()
        write.start()
    for copy in writes:
        copy.wait()


def per_device(
    inputs,
    queries,
    key_rows,
    values,
    norm_gain,
    cotangent,
    adapter_down,
    adapter_up,
    moment_down,
    moment_up,
    noise_down,
    noise_up,
):
    args = (
        inputs,
        queries,
        key_rows,
        values,
        norm_gain.reshape(1, COLS),
        cotangent,
        adapter_down,
        adapter_up,
        moment_down,
        moment_up,
        noise_down,
        noise_up,
    )
    out_shape = (
        jax.ShapeDtypeStruct((TOK, COLS), BF16),
        jax.ShapeDtypeStruct((RANK, FEATS), F32),
        jax.ShapeDtypeStruct((RANK, FEATS), F32),
        jax.ShapeDtypeStruct((RANK, COLS), F32),
        jax.ShapeDtypeStruct((RANK, COLS), F32),
    )

    def scan_bufs(n):
        whole = pltpu.VMEM((SIDE, n, HEAD), F32)
        return [whole] * 5

    scratch = [pltpu.VMEM(a.shape, a.dtype) for a in args]
    scratch += [pltpu.VMEM(s.shape, s.dtype) for s in out_shape]
    scratch += [
        pltpu.VMEM((TOK, COLS), BF16),
        pltpu.VMEM((TOK, COLS), BF16),
        pltpu.VMEM((TOK, COLS), BF16),
        pltpu.VMEM((HEADS, TOK, TOK), BF16),
        pltpu.VMEM((TOK, COLS), F32),
        pltpu.VMEM((HEADS, TOK, RANK), F32),
        pltpu.VMEM((TOK, COLS), BF16),
        pltpu.VMEM((RANK, TOK), BF16),
        pltpu.VMEM((TOK, RANK), BF16),
        pltpu.VMEM((RANK, TOK), F32),
    ]
    scratch += [pltpu.VMEM((HEADS, SIDE, HEAD // SIDE, HEAD), F32)] * 5
    for n in (16, 16, 16, 24):
        scratch += scan_bufs(n)
    half = RANK // 2
    for _ in range(2):
        scratch += [
            pltpu.VMEM((2, half, TOK), F32),
            pltpu.VMEM((half, TOK), F32),
            pltpu.VMEM((4, half, TOK), F32),
            pltpu.VMEM((2, half, TOK), F32),
        ]
    sem = pltpu.SemaphoreType.DMA
    scratch += [sem((12 + CHUNKS,)), sem((5,))]
    scratch += [sem((HEADS, SIDE))] * 6
    scratch += [sem((SIDE,))] * 24
    scratch += [sem((2,)), sem((8,)), sem((2,))] * 2
    scratch += [pltpu.VMEM((HEADS, RANK, TOK), BF16)]
    anywhere = pl.BlockSpec(memory_space=pl.ANY)
    results = pl.pallas_call(
        kernel,
        out_shape=out_shape,
        in_specs=[anywhere] * len(args),
        out_specs=(anywhere,) * len(out_shape),
        scratch_shapes=scratch,
        compiler_params=pltpu.CompilerParams(
            collective_id=0, has_side_effects=True, vmem_limit_bytes=60 * 2**20
        ),
        name="fused_update",
    )(*args)
    return pl.pallas_call(
        write_out,
        out_shape=out_shape,
        in_specs=[anywhere] * len(out_shape),
        out_specs=(anywhere,) * len(out_shape),
        scratch_shapes=[pltpu.VMEM(s.shape, s.dtype) for s in out_shape] + [sem((2, 8))],
        compiler_params=pltpu.CompilerParams(vmem_limit_bytes=60 * 2**20),
        name="write_out",
    )(*results)


def solution(mesh):
    return jax.shard_map(
        per_device,
        mesh=mesh,
        in_specs=(
            P("seq", "mp"),
            P("seq", "mp"),
            P("seq", "mp"),
            P("seq", "mp"),
            P("mp"),
            P("seq", "mp"),
            P(None, "mp"),
            P(None, "mp"),
            P(None, "mp"),
            P(None, "mp"),
            P(None, "mp"),
            P(None, "mp"),
        ),
        out_specs=(P("seq", "mp"), P(None, "mp"), P(None, "mp"), P(None, "mp"), P(None, "mp")),
        check_vma=False,
    )
```
